256 devices in a mesh: dp: 8 (over z_lo, y), tensor: 32 (over x, z_hi, core).
Axes of the slice: x: 4, y: 4, z: 8 (z_hi: 4, z_lo: 2; z = z_hi * 2 + z_lo), core: 2. Of those that a mesh axis runs over, the one named last changes fastest.
Arguments:
- tokens: bfloat16 [2048, 10240], P(('dp', 'tensor')), may hold values from -24 to 24
- cotangent: bfloat16 [2048, 10240], P('dp', 'tensor'), may hold values from -0.59765625 to 0.59765625
- old_weight: bfloat16 [5120, 5120], P('tensor'), may hold values from -0.078125 to 0.078125
- old_first: float32 [5120, 5120], P('tensor'), may hold values from -6 to 6
- old_second: float32 [5120, 5120], P('tensor'), may hold values from 0.25 to 4
- row_source: int32 [5120], replicated, may hold values from 0 to 5119
- col_source: int32 [5120], replicated, may hold values from 0 to 5119
- row_level: int32 [5120], replicated, may hold values from 0 to 4
- col_level: int32 [5120], replicated, may hold values from 0 to 4
Outputs:
- activation: bfloat16 [2048, 10240], P('dp', 'tensor')
- new_weight: bfloat16 [10240, 10240], P('dp', 'tensor')
- new_first: float32 [10240, 10240], P('dp', 'tensor')
- new_second: float32 [10240, 10240], P('dp', 'tensor')
The draws below stay inside these ranges and needn't reach their ends.
All inputs are finite; a program needn't handle non-finite values.
Results may differ from the reference program's by a relative error of at most 0.014.
Values may be sent and summed in bfloat16 or wider, within the bound.
No kernel may reach another device: no remote copies, remote signals or barrier semaphores. Data moves between devices by JAX's collectives and lax.ppermute only.
A program may use at most 128 MiB of HBM per device.

```python
import math
import jax
import jax.numpy as jnp
from jax import lax

D0 = 5120
D1 = 10240
TOK_GRP = 256
TOKENS = 2048
N_DP = 8


def with_ends(result, key, low, high):
    index_at = [jax.random.randint(jax.random.fold_in(key, axis), (), 0, length) for axis, length in enumerate(result.shape)]
    main_axis = result.shape.index(max(result.shape))
    beside = index_at[:main_axis] + [(index_at[main_axis] + 1) % result.shape[main_axis]] + index_at[main_axis + 1:]
    return result.at[tuple(index_at)].set(low).at[tuple(beside)].set(high)


def strengthened(result, key, source, target, parts, factor):
    def block_of(axis_at):
        return (jnp.arange(result.shape[axis_at]) // (result.shape[axis_at] // parts)).reshape((-1,) + (1,) * (result.ndim - 1 - axis_at))

    near = jax.random.permutation(key, parts)[block_of(target)]
    second = (block_of(target) + parts // 2) % parts
    return jnp.where((block_of(source) == near) | (block_of(source) == second), factor * result, result)


def steps_of(own_key, shape, shards, smallest, top_value):
    loudness, own = 1.0, jax.random.fold_in(own_key, 6)
    for position, shards_of in shards:
        heights = jnp.exp(jax.random.uniform(jax.random.fold_in(own, position), (shards_of,), jnp.float32, smallest / len(shards), top_value / len(shards)))
        loudness = loudness * jnp.repeat(heights, shape[position] // shards_of).reshape([-1 if axis == position else 1 for axis in range(len(shape))])
    return loudness


def gaussian(key, extent, deviation, reach, shards=(), kind=jnp.bfloat16):
    drawn = jax.random.normal(key, extent, jnp.float32) * deviation
    if len(shards) > 0:
        drawn = steps_of(key, extent, shards, -0.22, 0.18) * drawn
    return jnp.clip(drawn, min=-reach, max=reach).astype(kind)


def heavy_noise(own_key, extent, scale, bound, pieces, heavy, kind=jnp.bfloat16):
    array = scale * jax.random.normal(own_key, extent, jnp.float32)
    if pieces:
        array = array * steps_of(own_key, extent, pieces, -0.22, 0.18)
    return jnp.clip(strengthened(array, jax.random.fold_in(own_key, 3), *heavy), -bound, bound).astype(kind)


def setup_inputs(seed: int = 0) -> dict:
    arg_keys = jax.random.split(jax.random.key(seed), 10)
    tokens = heavy_noise(arg_keys[0], (TOKENS, D1), 1.0, 24.0, ((0, 256),), (0, 1, 256, 6.0))
    cotangent = gaussian(arg_keys[1], (TOKENS, D1), 0.09, 0.59765625, ((0, 8), (1, 32)))
    old_weight = gaussian(arg_keys[2], (D0, D0), D0 ** -0.5, 0.078125, ((0, 32),))
    old_first = gaussian(arg_keys[3], (D0, D0), 1.0, 6.0, ((0, 32),), jnp.float32)
    old_second = jnp.clip(jnp.exp(math.log(4.0) - 2.7725887 * jax.random.uniform(arg_keys[4], (D0, D0), jnp.float32) ** steps_of(arg_keys[4], (D0, D0), ((0, 32),), -0.2, 0.2)), 0.25, 4.0)
    row_source = with_ends(jax.random.randint(arg_keys[5], (D1 - D0,), 0, D0), jax.random.fold_in(arg_keys[5], 1), 0, D0 - 1).astype(jnp.int32)
    col_source = with_ends(jax.random.randint(arg_keys[6], (D1 - D0,), 0, D0), jax.random.fold_in(arg_keys[6], 1), 0, D0 - 1).astype(jnp.int32)
    row_level = with_ends(jax.random.randint(arg_keys[7], (D1 - D0,), 0, 5), jax.random.fold_in(arg_keys[7], 1), 0, 4).astype(jnp.int32)
    col_level = with_ends(jax.random.randint(arg_keys[8], (D1 - D0,), 0, 5), jax.random.fold_in(arg_keys[8], 1), 0, 4).astype(jnp.int32)
    return dict(tokens=tokens, cotangent=cotangent, old_weight=old_weight, old_first=old_first, old_second=old_second, row_source=row_source, col_source=col_source, row_level=row_level, col_level=col_level)


beta_one = 0.9
beta_two = 0.95
adam_eps = 1e-08
learn_rate = 0.01
weight_decay = 0.1
adam_step = 1000.0

def growth_maps(row_source, col_source, row_level, col_level, old_width):
    identity = jnp.arange(old_width, dtype=jnp.int32)
    row_map = jnp.concatenate([identity, row_source.astype(jnp.int32)])
    col_map = jnp.concatenate([identity, col_source.astype(jnp.int32)])
    unit_scale = jnp.ones((old_width,), jnp.float32)
    row_scale = jnp.concatenate([unit_scale, (row_level.astype(jnp.float32) + 1.0) / 5.0])
    col_scale = jnp.concatenate([unit_scale, (col_level.astype(jnp.float32) + 1.0) / 5.0])
    return (row_map, col_map, row_scale, col_scale)

def activate(values):
    return jax.nn.gelu(values, approximate=True)

def adam_update(weight_rows, first_moment, second_moment, gradient):
    weight_float = weight_rows.astype(jnp.float32)
    new_first = beta_one * first_moment + (1.0 - beta_one) * gradient
    new_second = beta_two * second_moment + (1.0 - beta_two) * gradient * gradient
    first_corr = 1.0 - beta_one ** adam_step
    second_corr = 1.0 - beta_two ** adam_step
    update = new_first / first_corr / (jnp.sqrt(new_second / second_corr) + adam_eps) + weight_decay * weight_float
    new_weight = (weight_float - learn_rate * update).astype(jnp.bfloat16)
    return (new_weight, new_first, new_second)

def reference(tokens, cotangent, old_weight, old_first, old_second, row_source, col_source, row_level, col_level):
    row_map, col_map, row_scale, col_scale = growth_maps(row_source, col_source, row_level, col_level, D0)
    copied = jnp.take(jnp.take(old_weight, row_map, axis=0), col_map, axis=1)
    grown_weight = (copied.astype(jnp.float32) * row_scale[:, None] * col_scale[None, :]).astype(jnp.bfloat16)
    grown_first = jnp.take(jnp.take(old_first, row_map, axis=0), col_map, axis=1)
    grown_second = jnp.take(jnp.take(old_second, row_map, axis=0), col_map, axis=1)
    hidden = jnp.dot(tokens, grown_weight, preferred_element_type=jnp.float32)
    activation = activate(hidden).astype(jnp.bfloat16)
    _, pullback = jax.vjp(activate, hidden)
    hidden_grad = pullback(cotangent.astype(jnp.float32))[0].astype(jnp.bfloat16)
    token_groups = tokens.reshape(N_DP, TOK_GRP, D1)
    grad_groups = hidden_grad.reshape(N_DP, TOK_GRP, D1)

    def add_group(running, pair):
        group_term = lax.dot_general(pair[0], pair[1], (((0,), (0,)), ((), ())), preferred_element_type=jnp.float32)
        rounded = lax.optimization_barrier(group_term.astype(jnp.bfloat16))
        return (running + rounded.astype(jnp.float32), None)
    gradient, _ = lax.scan(add_group, jnp.zeros((D1, D1), jnp.float32), (token_groups, grad_groups))
    new_weight, new_first, new_second = adam_update(grown_weight, grown_first, grown_second, gradient)
    return (activation, new_weight, new_first, new_second)
```

```python
import functools

import jax
import jax.numpy as jnp
from jax import lax
from jax.experimental import pallas as pl
from jax.experimental.pallas import tpu as pltpu
from jax.sharding import PartitionSpec as P

beta_one = 0.9
beta_two = 0.95
adam_eps = 1e-08
learn_rate = 0.01
weight_decay = 0.1
adam_step = 1000.0

LANES = 128
F32 = jnp.float32
BF16 = jnp.bfloat16
VMEM_BYTES = 56 * 1024 * 1024


def growth_maps(row_source, col_source, row_level, col_level, old_width):
    identity = jnp.arange(old_width, dtype=jnp.int32)
    row_map = jnp.concatenate([identity, row_source])
    col_map = jnp.concatenate([identity, col_source])
    unit_scale = jnp.ones((old_width,), F32)
    row_scale = jnp.concatenate([unit_scale, (row_level.astype(F32) + 1.0) / 5.0])
    col_scale = jnp.concatenate([unit_scale, (col_level.astype(F32) + 1.0) / 5.0])
    return (row_map, col_map, row_scale, col_scale)


def activate(values):
    return jax.nn.gelu(values, approximate=True)


def chosen(index_row, depth, start=0):
    at = lax.broadcasted_iota(jnp.int32, (depth, index_row.shape[1]), 0) + start
    return jnp.where(at == index_row, 1.0, 0.0).astype(BF16)


def dot(a, b):
    return jnp.dot(a, b, preferred_element_type=F32)


def column_kernel(slabs_step, copy_ref, own_ref, place_ref, w_ref, m_ref, v_ref, out_ref, total, own_place):
    step = pl.program_id(0)
    rows, depth = w_ref.shape
    parts = [w_ref[...], m_ref[...].astype(BF16), v_ref[...].astype(BF16)]

    @pl.when(step == 0)
    def _():
        for k in range(3):
            own_place[k] = chosen(own_ref[k : k + 1, :], depth)

    same = functools.reduce(
        lambda a, b: a + b,
        [dot(part, own_place[k]) for k, part in enumerate(parts)],
    ).astype(BF16)
    for j in range(slabs_step):
        out_ref[step * slabs_step + j] = same[:, j * LANES : (j + 1) * LANES]
    picked = dot(jnp.concatenate(parts, axis=0), chosen(copy_ref[...], depth, step * depth))

    @pl.when(step == 0)
    def _():
        total[...] = picked

    @pl.when(step > 0)
    def _():
        total[...] += picked

    @pl.when(step == pl.num_programs(0) - 1)
    def _():
        half = out_ref.shape[0] // 2
        width = total.shape[1]
        held = [total[k * rows : (k + 1) * rows, :].astype(BF16) for k in range(3)]
        spread = functools.reduce(
            lambda a, b: a + b,
            [dot(part, chosen(place_ref[k : k + 1, :], width)) for k, part in enumerate(held)],
        ).astype(BF16)
        for j in range(half):
            out_ref[half + j] = spread[:, j * LANES : (j + 1) * LANES]


def grow_columns(old_weight, old_first, old_second, col_source, slabs, slab_width, pieces, piece_at):
    rows, old_width = old_weight.shape
    piece = slab_width // pieces
    half = slabs // 2
    slabs_step = 2
    depth = slabs_step * slab_width
    copy_index = lax.dynamic_slice_in_dim(
        col_source.reshape(half, pieces, piece), piece_at, 1, 1
    ).reshape(1, half * piece)
    lane = jnp.arange(LANES, dtype=jnp.int32)[None, :] - piece * jnp.arange(3, dtype=jnp.int32)[:, None]
    inside = (lane >= 0) & (lane < piece)

    def spread_index(count, stride, offset):
        slab = jnp.arange(count, dtype=jnp.int32)[None, :, None] * stride + offset
        return jnp.where(inside[:, None, :], lane[:, None, :] + slab, -1).reshape(3, count * LANES)

    own_index = spread_index(slabs_step, slab_width, piece_at * piece)
    place_index = spread_index(half, piece, 0)
    return pl.pallas_call(
        functools.partial(column_kernel, slabs_step),
        grid=(half // slabs_step,),
        in_specs=[
            pl.BlockSpec((1, half * piece), lambda s: (0, 0)),
            pl.BlockSpec((3, slabs_step * LANES), lambda s: (0, 0)),
            pl.BlockSpec((3, half * LANES), lambda s: (0, 0)),
            pl.BlockSpec((rows, depth), lambda s: (0, s)),
            pl.BlockSpec((rows, depth), lambda s: (0, s)),
            pl.BlockSpec((rows, depth), lambda s: (0, s)),
        ],
        out_specs=pl.BlockSpec((slabs, rows, LANES), lambda s: (0, 0, 0)),
        out_shape=jax.ShapeDtypeStruct((slabs, rows, LANES), BF16),
        scratch_shapes=[
            pltpu.VMEM((3 * rows, half * piece), F32),
            pltpu.VMEM((3, depth, slabs_step * LANES), BF16),
        ],
        compiler_params=pltpu.CompilerParams(vmem_limit_bytes=VMEM_BYTES),
        cost_estimate=pl.CostEstimate(flops=1000, bytes_accessed=1000, transcendentals=0),
        name="grow_columns",
    )(copy_index, own_index, place_index, old_weight, old_first, old_second)


def row_kernel(index_ref, in_ref, out_ref, wide, picked):
    old = in_ref.shape[0]
    chunk = 512
    for c in range(0, old, chunk):
        part = in_ref[c : c + chunk, :]
        out_ref[c : c + chunk, :] = part
        wide[c : c + chunk, :] = part.astype(F32)

    def body(c, carry):
        for i in range(32):
            at = c * 32 + i
            picked[pl.ds(at, 1), :] = wide[pl.ds(index_ref[at], 1), :]
        return carry

    lax.fori_loop(0, old // 32, body, 0)
    for c in range(0, old, chunk):
        out_ref[old + c : old + c + chunk, :] = picked[c : c + chunk, :].astype(BF16)


def grow_rows(columns, row_source):
    old = columns.shape[0]
    return pl.pallas_call(
        row_kernel,
        in_specs=[
            pl.BlockSpec(memory_space=pltpu.SMEM),
            pl.BlockSpec(memory_space=pltpu.VMEM),
        ],
        out_specs=pl.BlockSpec(memory_space=pltpu.VMEM),
        out_shape=jax.ShapeDtypeStruct((2 * old, LANES), BF16),
        scratch_shapes=[pltpu.VMEM((old, LANES), F32), pltpu.VMEM((old, LANES), F32)],
        compiler_params=pltpu.CompilerParams(vmem_limit_bytes=VMEM_BYTES),
        cost_estimate=pl.CostEstimate(flops=1000, bytes_accessed=1000, transcendentals=0),
        name="grow_rows",
    )(row_source, columns)


def assemble(blocks_ref, array_at, piece, slab_width):
    pieces = blocks_ref.shape[0]
    row = lax.broadcasted_iota(jnp.int32, (slab_width, LANES), 0)
    at = lax.broadcasted_iota(jnp.int32, (slab_width, LANES), 1) - array_at * piece
    inside = (at >= 0) & (at < piece)
    place = jnp.concatenate(
        [jnp.where(inside & (d * piece + at == row), 1.0, 0.0).astype(BF16) for d in range(pieces)], axis=1
    )
    block = jnp.concatenate([blocks_ref[d] for d in range(pieces)], axis=1)
    return lax.dot_general(place, block, (((1,), (1,)), ((), ())), preferred_element_type=F32)


def weight_kernel(piece, blocks_ref, row_scale_ref, col_scale_ref, weight_ref):
    copied = assemble(blocks_ref, 0, piece, weight_ref.shape[0])
    weight_ref[...] = (copied * row_scale_ref[...] * col_scale_ref[...]).astype(BF16)


def moments_kernel(piece, blocks_ref, first_ref, second_ref):
    for a, ref in enumerate((first_ref, second_ref)):
        ref[...] = assemble(blocks_ref, a + 1, piece, ref.shape[0]).astype(BF16)


def grown_block(kernel, operands, results, block_rows, slab_width, piece):
    shape = jax.ShapeDtypeStruct((slab_width, block_rows), BF16)
    return pl.pallas_call(
        functools.partial(kernel, piece),
        in_specs=[pl.BlockSpec(memory_space=pltpu.VMEM)] * len(operands),
        out_specs=[pl.BlockSpec(memory_space=pltpu.VMEM)] * results,
        out_shape=[shape] * results,
        compiler_params=pltpu.CompilerParams(vmem_limit_bytes=VMEM_BYTES),
        cost_estimate=pl.CostEstimate(flops=1000, bytes_accessed=1000, transcendentals=0),
        name="grown_block_%d" % results,
    )(*operands)


def forward_kernel(place_ref, *refs):
    parts, weight_ref, out_ref = refs[:-2], refs[-2], refs[-1]
    step = pl.program_id(0)
    half = pl.num_programs(0)
    core = place_ref[1]
    count = len(parts) // 2
    for refs_of, at in ((parts[:count], core), (parts[count:], 1 - core)):
        group = jnp.concatenate([ref[...].reshape(-1, ref.shape[-1]) for ref in refs_of], axis=0)
        out_ref[at * half + step] = lax.dot_general(
            weight_ref[...], group, (((1,), (1,)), ((), ())), preferred_element_type=F32
        ).astype(BF16)


def forward(place, parts, weight, groups):
    near, half, chip_rows, block_rows = parts[0].shape
    shape = (groups, weight.shape[0], len(parts) // 2 * near * chip_rows)
    tokens = pl.BlockSpec((near, 1, chip_rows, block_rows), lambda s: (0, s, 0, 0))
    return pl.pallas_call(
        forward_kernel,
        grid=(half,),
        in_specs=[pl.BlockSpec(memory_space=pltpu.SMEM)]
        + [tokens] * len(parts)
        + [pl.BlockSpec(weight.shape, lambda s: (0, 0))],
        out_specs=pl.BlockSpec(shape, lambda s: (0, 0, 0)),
        out_shape=jax.ShapeDtypeStruct(shape, BF16),
        compiler_params=pltpu.CompilerParams(vmem_limit_bytes=VMEM_BYTES),
        cost_estimate=pl.CostEstimate(flops=1000, bytes_accessed=1000, transcendentals=0),
        name="forward_terms",
    )(place, *parts, weight)


def adam_kernel(groups, place_ref, *refs):
    parts, grads, refs = refs[: -groups - 7], refs[-groups - 7 : -7], refs[-7:]
    first_ref, second_ref, weight_ref, new_weight_ref, new_first_ref, new_second_ref, held = refs
    step_rows = weight_ref.shape[1]
    half = parts[0].shape[1]
    core = place_ref[1]
    count = len(parts) // 2

    @pl.when(pl.program_id(0) == 0)
    def _():
        for k, ref in enumerate(grads):
            held[jnp.bitwise_xor(place_ref[0], k)] = ref[...]

    gradient = None
    for refs_of, at in ((parts[:count], core), (parts[count:], 1 - core)):
        for j in range(half):
            group = jnp.concatenate([ref[:, j].reshape(-1, step_rows) for ref in refs_of], axis=0)
            term = dot(held[at * half + j], group)
            gradient = term if gradient is None else gradient + term
    weight = weight_ref[...].astype(F32)
    new_first = beta_one * first_ref[...].astype(F32) + (1.0 - beta_one) * gradient
    new_second = beta_two * second_ref[...].astype(F32) + (1.0 - beta_two) * gradient * gradient
    first_corr = 1.0 - beta_one**adam_step
    second_corr = 1.0 - beta_two**adam_step
    update = (
        new_first * (1.0 / first_corr) / (jnp.sqrt(new_second * (1.0 / second_corr)) + adam_eps)
        + weight_decay * weight
    )
    new_weight_ref[...] = (weight - learn_rate * update).astype(BF16)
    new_first_ref[...] = new_first
    new_second_ref[...] = new_second


def backward(place, parts, grads, first, second, weight):
    near, half, chip_rows, block_rows = parts[0].shape
    slab_width = weight.shape[0]
    step_rows = 256
    tokens = pl.BlockSpec((near, half, chip_rows, step_rows), lambda s: (0, 0, 0, s))
    block = pl.BlockSpec((slab_width, step_rows), lambda s: (0, s))
    return pl.pallas_call(
        functools.partial(adam_kernel, len(grads)),
        grid=(block_rows // step_rows,),
        in_specs=[pl.BlockSpec(memory_space=pltpu.SMEM)]
        + [tokens] * len(parts)
        + [pl.BlockSpec(grads[0].shape, lambda s: (0, 0))] * len(grads)
        + [block, block, block],
        out_specs=[block, block, block],
        out_shape=[
            jax.ShapeDtypeStruct((slab_width, block_rows), BF16),
            jax.ShapeDtypeStruct((slab_width, block_rows), F32),
            jax.ShapeDtypeStruct((slab_width, block_rows), F32),
        ],
        scratch_shapes=[pltpu.VMEM((len(grads),) + grads[0].shape, BF16)],
        compiler_params=pltpu.CompilerParams(vmem_limit_bytes=VMEM_BYTES),
        cost_estimate=pl.CostEstimate(flops=1000, bytes_accessed=1000, transcendentals=0),
        name="gradient_adam",
    )(place, *parts, *grads, first, second, weight)


DIM_X, DIM_Z = 4, 4


def shifted(dx, dz, dc):
    places = [(x, z, c) for x in range(DIM_X) for z in range(DIM_Z) for c in range(2)]

    def at(x, z, c):
        return ((x % DIM_X) * DIM_Z + z % DIM_Z) * 2 + c % 2

    return [(at(x, z, c), at(x + dx, z + dz, c + dc)) for x, z, c in places]


def stack_kernel(*refs):
    for k, ref in enumerate(refs[:-1]):
        refs[-1][k] = ref[0]


def stacked(values):
    shape = (len(values),) + values[0].shape[1:]
    return pl.pallas_call(
        stack_kernel,
        in_specs=[pl.BlockSpec(memory_space=pltpu.VMEM)] * len(values),
        out_specs=pl.BlockSpec(memory_space=pltpu.VMEM),
        out_shape=jax.ShapeDtypeStruct(shape, values[0].dtype),
        compiler_params=pltpu.CompilerParams(vmem_limit_bytes=VMEM_BYTES),
        cost_estimate=pl.CostEstimate(flops=1000, bytes_accessed=1000, transcendentals=0),
        name="stack_tokens",
    )(*values)


def chip_tokens(part, core):
    groups, rows, block_rows = part.shape
    half = groups // 2
    mine = lax.dynamic_slice_in_dim(part, core * half, half, 0)
    away = lax.dynamic_slice_in_dim(part, (1 - core) * half, half, 0)
    theirs = lax.ppermute(away, "tensor", shifted(0, 0, 1))
    chip = jnp.stack([jnp.where(core == 0, mine, theirs), jnp.where(core == 0, theirs, mine)], axis=1)
    return chip.reshape(1, half, 2 * rows, block_rows)


def to_groups(values):
    groups = lax.axis_size("dp")
    return [values] + [lax.ppermute(values, "dp", [(i, i ^ k) for i in range(groups)]) for k in range(1, groups)]


def in_order(values, *others):
    return lax.optimization_barrier((values, *others))


def shards(tokens, cotangent, old_weight, old_first, old_second, row_source, col_source, row_level, col_level):
    slabs = lax.axis_size("tensor")
    groups = lax.axis_size("dp")
    slab_at, group_at = lax.axis_index("tensor"), lax.axis_index("dp")
    core = slab_at % 2
    place = jnp.stack([group_at, core]).astype(jnp.int32)
    rows = tokens.shape[0]
    old_width = old_weight.shape[1]
    new_width = old_width + row_source.shape[0]
    slab_width = new_width // slabs
    block_rows = new_width // groups
    piece = slab_width // groups
    _, _, row_scale, col_scale = growth_maps(row_source, col_source, row_level, col_level, old_width)
    row_scale = lax.dynamic_slice_in_dim(row_scale, group_at * block_rows, block_rows)[None, :]
    col_scale = lax.dynamic_slice_in_dim(col_scale, slab_at * slab_width, slab_width)[:, None]

    def exchange(values, axis):
        return lax.all_to_all(values, axis, split_axis=0, concat_axis=0, tiled=True)

    chip_at = slab_at // 2
    lane = jnp.arange(slabs * rows, dtype=jnp.int32)
    away, within = lane // (2 * rows), lane % (2 * rows)
    chip_x = (chip_at // DIM_Z - away // DIM_Z) % DIM_X
    chip_z = (chip_at % DIM_Z - away % DIM_Z) % DIM_Z
    real = (chip_x * DIM_Z + chip_z) * 2 * rows + within
    to_real = (real[:, None] == lane[None, :]).astype(BF16)

    part = lax.all_to_all(tokens, "dp", split_axis=1, concat_axis=0, tiled=True)
    columns = grow_columns(old_weight, old_first, old_second, col_source, slabs, slab_width, groups, group_at)
    part, columns = in_order(part, columns)
    columns = exchange(columns, "tensor")
    chip = chip_tokens(part.reshape(groups, rows, block_rows), core)
    along_z = [chip] + [lax.ppermute(chip, "tensor", shifted(0, k, 0)) for k in range(1, DIM_Z)]
    along_z = stacked(along_z)
    own = [along_z] + [lax.ppermute(along_z, "tensor", shifted(k, 0, 0)) for k in range(1, DIM_X)]
    grown = grow_rows(columns.reshape(old_width, LANES), row_source)
    blocks = exchange(grown.reshape(groups, block_rows, LANES), "dp")
    blocks, *own = in_order(blocks, *own)
    parts = own + [lax.ppermute(values, "tensor", shifted(0, 0, 1)) for values in own]
    (weight,) = grown_block(weight_kernel, (blocks, row_scale, col_scale), 1, block_rows, slab_width, piece)

    terms = exchange(forward(place, parts, weight, groups), "dp")
    first, second = grown_block(moments_kernel, (blocks,), 2, block_rows, slab_width, piece)
    terms, first, second = in_order(terms, first, second)
    turned_grad = dot(cotangent.T, to_real.T)
    hidden = terms.astype(F32).sum(axis=0)
    activation = activate(hidden).astype(BF16)
    _, pullback = jax.vjp(activate, hidden)
    hidden_grad = pullback(turned_grad)[0].astype(BF16)
    activation = dot(activation, to_real).astype(BF16)

    grads = to_groups(hidden_grad)
    news = backward(place, parts, grads, first, second, weight)
    return (activation.T,) + tuple(new.T for new in news)


def solution(mesh):
    placed = (
        P(("dp", "tensor"), None),
        P("dp", "tensor"),
        P("tensor", None),
        P("tensor", None),
        P("tensor", None),
        P(),
        P(),
        P(),
        P(),
    )
    return jax.shard_map(
        shards,
        mesh=mesh,
        in_specs=placed,
        out_specs=(P("dp", "tensor"), P("dp", "tensor"), P("dp", "tensor"), P("dp", "tensor")),
        check_vma=False,
    )
```

```python
import functools

import jax
import jax.numpy as jnp
from jax import lax
from jax.experimental import pallas as pl
from jax.experimental.pallas import tpu as pltpu
from jax.sharding import PartitionSpec as P

beta_one = 0.9
beta_two = 0.95
adam_eps = 1e-08
learn_rate = 0.01
weight_decay = 0.1
adam_step = 1000.0

LANES = 128
F32 = jnp.float32
BF16 = jnp.bfloat16
VMEM_BYTES = 56 * 1024 * 1024


def growth_maps(row_source, col_source, row_level, col_level, old_width):
    identity = jnp.arange(old_width, dtype=jnp.int32)
    row_map = jnp.concatenate([identity, row_source])
    col_map = jnp.concatenate([identity, col_source])
    unit_scale = jnp.ones((old_width,), F32)
    row_scale = jnp.concatenate([unit_scale, (row_level.astype(F32) + 1.0) / 5.0])
    col_scale = jnp.concatenate([unit_scale, (col_level.astype(F32) + 1.0) / 5.0])
    return (row_map, col_map, row_scale, col_scale)


def activate(values):
    return jax.nn.gelu(values, approximate=True)


def chosen(index_row, depth, start=0):
    at = lax.broadcasted_iota(jnp.int32, (depth, index_row.shape[1]), 0) + start
    return jnp.where(at == index_row, 1.0, 0.0).astype(BF16)


def dot(a, b):
    return jnp.dot(a, b, preferred_element_type=F32)


def column_kernel(slabs_step, piece, copy_ref, own_ref, place_ref, w_ref, m_ref, v_ref, out_ref, total, own_place):
    step = pl.program_id(0)
    rows, depth = w_ref.shape
    parts = [w_ref[...], m_ref[...].astype(BF16), v_ref[...].astype(BF16)]

    @pl.when(step == 0)
    def _():
        for k in range(3):
            own_place[k] = chosen(own_ref[k : k + 1, :], depth)

    same = functools.reduce(
        lambda a, b: a + b,
        [dot(part, own_place[k]) for k, part in enumerate(parts)],
    ).astype(BF16)
    for j in range(slabs_step):
        out_ref[step * slabs_step + j] = same[:, j * LANES : (j + 1) * LANES]
    picked = dot(jnp.concatenate(parts, axis=0), chosen(copy_ref[...], depth, step * depth))

    @pl.when(step == 0)
    def _():
        total[...] = picked

    @pl.when(step > 0)
    def _():
        total[...] += picked

    @pl.when(step == pl.num_programs(0) - 1)
    def _():
        half = out_ref.shape[0] // 2
        width = total.shape[1]
        window = 2 * LANES
        held = [total[k * rows : (k + 1) * rows, :].astype(BF16) for k in range(3)]
        starts = [min(j * piece // LANES * LANES, width - window) for j in range(half)]
        for start in sorted(set(starts)):
            slabs = [j for j in range(half) if starts[j] == start]
            lanes = slice(slabs[0] * LANES, (slabs[-1] + 1) * LANES)
            spread = functools.reduce(
                lambda a, b: a + b,
                [
                    dot(part[:, start : start + window], chosen(place_ref[k : k + 1, lanes], window, start))
                    for k, part in enumerate(held)
                ],
            ).astype(BF16)
            for i, j in enumerate(slabs):
                out_ref[half + j] = spread[:, i * LANES : (i + 1) * LANES]


def grow_columns(old_weight, old_first, old_second, col_source, slabs, slab_width, pieces, piece_at):
    rows, old_width = old_weight.shape
    piece = slab_width // pieces
    half = slabs // 2
    slabs_step = 2
    depth = slabs_step * slab_width
    copy_index = lax.dynamic_slice_in_dim(
        col_source.reshape(half, pieces, piece), piece_at, 1, 1
    ).reshape(1, half * piece)
    lane = jnp.arange(LANES, dtype=jnp.int32)[None, :] - piece * jnp.arange(3, dtype=jnp.int32)[:, None]
    inside = (lane >= 0) & (lane < piece)

    def spread_index(count, stride, offset):
        slab = jnp.arange(count, dtype=jnp.int32)[None, :, None] * stride + offset
        return jnp.where(inside[:, None, :], lane[:, None, :] + slab, -1).reshape(3, count * LANES)

    own_index = spread_index(slabs_step, slab_width, piece_at * piece)
    place_index = spread_index(half, piece, 0)
    return pl.pallas_call(
        functools.partial(column_kernel, slabs_step, piece),
        grid=(half // slabs_step,),
        in_specs=[
            pl.BlockSpec((1, half * piece), lambda s: (0, 0)),
            pl.BlockSpec((3, slabs_step * LANES), lambda s: (0, 0)),
            pl.BlockSpec((3, half * LANES), lambda s: (0, 0)),
            pl.BlockSpec((rows, depth), lambda s: (0, s)),
            pl.BlockSpec((rows, depth), lambda s: (0, s)),
            pl.BlockSpec((rows, depth), lambda s: (0, s)),
        ],
        out_specs=pl.BlockSpec((slabs, rows, LANES), lambda s: (0, 0, 0)),
        out_shape=jax.ShapeDtypeStruct((slabs, rows, LANES), BF16),
        scratch_shapes=[
            pltpu.VMEM((3 * rows, half * piece), F32),
            pltpu.VMEM((3, depth, slabs_step * LANES), BF16),
        ],
        compiler_params=pltpu.CompilerParams(vmem_limit_bytes=VMEM_BYTES),
        cost_estimate=pl.CostEstimate(flops=1000, bytes_accessed=1000, transcendentals=0),
        name="grow_columns",
    )(copy_index, own_index, place_index, old_weight, old_first, old_second)


def row_kernel(index_ref, in_ref, out_ref, wide, picked):
    old = in_ref.shape[0]
    chunk = 512
    for c in range(0, old, chunk):
        part = in_ref[c : c + chunk, :]
        out_ref[c : c + chunk, :] = part
        wide[c : c + chunk, :] = part.astype(F32)

    def body(c, carry):
        for i in range(32):
            at = c * 32 + i
            picked[pl.ds(at, 1), :] = wide[pl.ds(index_ref[at], 1), :]
        return carry

    lax.fori_loop(0, old // 32, body, 0)
    for c in range(0, old, chunk):
        out_ref[old + c : old + c + chunk, :] = picked[c : c + chunk, :].astype(BF16)


def grow_rows(columns, row_source):
    old = columns.shape[0]
    return pl.pallas_call(
        row_kernel,
        in_specs=[
            pl.BlockSpec(memory_space=pltpu.SMEM),
            pl.BlockSpec(memory_space=pltpu.VMEM),
        ],
        out_specs=pl.BlockSpec(memory_space=pltpu.VMEM),
        out_shape=jax.ShapeDtypeStruct((2 * old, LANES), BF16),
        scratch_shapes=[pltpu.VMEM((old, LANES), F32), pltpu.VMEM((old, LANES), F32)],
        compiler_params=pltpu.CompilerParams(vmem_limit_bytes=VMEM_BYTES),
        cost_estimate=pl.CostEstimate(flops=1000, bytes_accessed=1000, transcendentals=0),
        name="grow_rows",
    )(row_source, columns)


def assemble(blocks_ref, array_at, piece, slab_width):
    pieces = blocks_ref.shape[0]
    row = lax.broadcasted_iota(jnp.int32, (slab_width, LANES), 0)
    at = lax.broadcasted_iota(jnp.int32, (slab_width, LANES), 1) - array_at * piece
    inside = (at >= 0) & (at < piece)
    place = jnp.concatenate(
        [jnp.where(inside & (d * piece + at == row), 1.0, 0.0).astype(BF16) for d in range(pieces)], axis=1
    )
    block = jnp.concatenate([blocks_ref[d] for d in range(pieces)], axis=1)
    return lax.dot_general(place, block, (((1,), (1,)), ((), ())), preferred_element_type=F32)


def weight_kernel(piece, blocks_ref, row_scale_ref, col_scale_ref, weight_ref):
    copied = assemble(blocks_ref, 0, piece, weight_ref.shape[0])
    weight_ref[...] = (copied * row_scale_ref[...] * col_scale_ref[...]).astype(BF16)


def moments_kernel(piece, blocks_ref, first_ref, second_ref):
    for a, ref in enumerate((first_ref, second_ref)):
        ref[...] = assemble(blocks_ref, a + 1, piece, ref.shape[0]).astype(BF16)


def grown_block(kernel, operands, results, block_rows, slab_width, piece):
    shape = jax.ShapeDtypeStruct((slab_width, block_rows), BF16)
    return pl.pallas_call(
        functools.partial(kernel, piece),
        in_specs=[pl.BlockSpec(memory_space=pltpu.VMEM)] * len(operands),
        out_specs=[pl.BlockSpec(memory_space=pltpu.VMEM)] * results,
        out_shape=[shape] * results,
        compiler_params=pltpu.CompilerParams(vmem_limit_bytes=VMEM_BYTES),
        cost_estimate=pl.CostEstimate(flops=1000, bytes_accessed=1000, transcendentals=0),
        name="grown_block_%d" % results,
    )(*operands)


def forward_kernel(place_ref, *refs):
    parts, weight_ref, out_ref = refs[:-2], refs[-2], refs[-1]
    step = pl.program_id(0)
    half = pl.num_programs(0)
    core = place_ref[1]
    both = [ref[...].reshape(-1, ref.shape[-1]) for ref in parts]
    term = lax.dot_general(
        weight_ref[...], jnp.concatenate(both, axis=0), (((1,), (1,)), ((), ())), preferred_element_type=F32
    ).astype(BF16)
    width = out_ref.shape[2]
    out_ref[core * half + step] = term[:, :width]
    out_ref[(1 - core) * half + step] = term[:, width:]


def forward(place, parts, weight, groups):
    near, half, chip_rows, block_rows = parts[0].shape
    shape = (groups, weight.shape[0], len(parts) // 2 * near * chip_rows)
    tokens = pl.BlockSpec((near, 1, chip_rows, block_rows), lambda s: (0, s, 0, 0))
    return pl.pallas_call(
        forward_kernel,
        grid=(half,),
        in_specs=[pl.BlockSpec(memory_space=pltpu.SMEM)]
        + [tokens] * len(parts)
        + [pl.BlockSpec(weight.shape, lambda s: (0, 0))],
        out_specs=pl.BlockSpec(shape, lambda s: (0, 0, 0)),
        out_shape=jax.ShapeDtypeStruct(shape, BF16),
        compiler_params=pltpu.CompilerParams(vmem_limit_bytes=VMEM_BYTES),
        cost_estimate=pl.CostEstimate(flops=1000, bytes_accessed=1000, transcendentals=0),
        name="forward_terms",
    )(place, *parts, weight)


def adam_kernel(groups, place_ref, *refs):
    parts, grads, refs = refs[: -groups - 7], refs[-groups - 7 : -7], refs[-7:]
    first_ref, second_ref, weight_ref, new_weight_ref, new_first_ref, new_second_ref, held = refs
    step_rows = weight_ref.shape[1]
    half = parts[0].shape[1]
    core = place_ref[1]
    count = len(parts) // 2

    @pl.when(pl.program_id(0) == 0)
    def _():
        for k, ref in enumerate(grads):
            held[jnp.bitwise_xor(place_ref[0], k)] = ref[...]

    grads_in_order, groups_in_order = [], []
    for refs_of, at in ((parts[:count], core), (parts[count:], 1 - core)):
        for j in range(half):
            grads_in_order.append(held[at * half + j])
            groups_in_order += [ref[:, j].reshape(-1, step_rows) for ref in refs_of]
    gradient = dot(jnp.concatenate(grads_in_order, axis=1), jnp.concatenate(groups_in_order, axis=0))
    weight = weight_ref[...].astype(F32)
    new_first = beta_one * first_ref[...].astype(F32) + (1.0 - beta_one) * gradient
    new_second = beta_two * second_ref[...].astype(F32) + (1.0 - beta_two) * gradient * gradient
    first_corr = 1.0 - beta_one**adam_step
    second_corr = 1.0 - beta_two**adam_step
    update = (
        new_first * (1.0 / first_corr) / (jnp.sqrt(new_second * (1.0 / second_corr)) + adam_eps)
        + weight_decay * weight
    )
    new_weight_ref[...] = (weight - learn_rate * update).astype(BF16)
    new_first_ref[...] = new_first
    new_second_ref[...] = new_second


def backward(place, parts, grads, first, second, weight):
    near, half, chip_rows, block_rows = parts[0].shape
    slab_width = weight.shape[0]
    step_rows = 256
    tokens = pl.BlockSpec((near, half, chip_rows, step_rows), lambda s: (0, 0, 0, s))
    block = pl.BlockSpec((slab_width, step_rows), lambda s: (0, s))
    return pl.pallas_call(
        functools.partial(adam_kernel, len(grads)),
        grid=(block_rows // step_rows,),
        in_specs=[pl.BlockSpec(memory_space=pltpu.SMEM)]
        + [tokens] * len(parts)
        + [pl.BlockSpec(grads[0].shape, lambda s: (0, 0))] * len(grads)
        + [block, block, block],
        out_specs=[block, block, block],
        out_shape=[
            jax.ShapeDtypeStruct((slab_width, block_rows), BF16),
            jax.ShapeDtypeStruct((slab_width, block_rows), F32),
            jax.ShapeDtypeStruct((slab_width, block_rows), F32),
        ],
        scratch_shapes=[pltpu.VMEM((len(grads),) + grads[0].shape, BF16)],
        compiler_params=pltpu.CompilerParams(vmem_limit_bytes=VMEM_BYTES),
        cost_estimate=pl.CostEstimate(flops=1000, bytes_accessed=1000, transcendentals=0),
        name="gradient_adam",
    )(place, *parts, *grads, first, second, weight)


DIM_X, DIM_Z = 4, 4


def shifted(dx, dz, dc):
    places = [(x, z, c) for x in range(DIM_X) for z in range(DIM_Z) for c in range(2)]

    def at(x, z, c):
        return ((x % DIM_X) * DIM_Z + z % DIM_Z) * 2 + c % 2

    return [(at(x, z, c), at(x + dx, z + dz, c + dc)) for x, z, c in places]


def stack_kernel(*refs):
    for k, ref in enumerate(refs[:-1]):
        refs[-1][k] = ref[0]


def stacked(values):
    shape = (len(values),) + values[0].shape[1:]
    return pl.pallas_call(
        stack_kernel,
        in_specs=[pl.BlockSpec(memory_space=pltpu.VMEM)] * len(values),
        out_specs=pl.BlockSpec(memory_space=pltpu.VMEM),
        out_shape=jax.ShapeDtypeStruct(shape, values[0].dtype),
        compiler_params=pltpu.CompilerParams(vmem_limit_bytes=VMEM_BYTES),
        cost_estimate=pl.CostEstimate(flops=1000, bytes_accessed=1000, transcendentals=0),
        name="stack_tokens",
    )(*values)


def chip_tokens(part, core):
    groups, rows, block_rows = part.shape
    half = groups // 2
    mine = lax.dynamic_slice_in_dim(part, core * half, half, 0)
    away = lax.dynamic_slice_in_dim(part, (1 - core) * half, half, 0)
    theirs = lax.ppermute(away, "tensor", shifted(0, 0, 1))
    chip = jnp.stack([jnp.where(core == 0, mine, theirs), jnp.where(core == 0, theirs, mine)], axis=1)
    return chip.reshape(1, half, 2 * rows, block_rows)


def to_groups(values):
    groups = lax.axis_size("dp")
    return [values] + [lax.ppermute(values, "dp", [(i, i ^ k) for i in range(groups)]) for k in range(1, groups)]


def in_order(values, *others):
    return lax.optimization_barrier((values, *others))


def shards(tokens, cotangent, old_weight, old_first, old_second, row_source, col_source, row_level, col_level):
    slabs = lax.axis_size("tensor")
    groups = lax.axis_size("dp")
    slab_at, group_at = lax.axis_index("tensor"), lax.axis_index("dp")
    core = slab_at % 2
    place = jnp.stack([group_at, core]).astype(jnp.int32)
    rows = tokens.shape[0]
    old_width = old_weight.shape[1]
    new_width = old_width + row_source.shape[0]
    slab_width = new_width // slabs
    block_rows = new_width // groups
    piece = slab_width // groups
    _, _, row_scale, col_scale = growth_maps(row_source, col_source, row_level, col_level, old_width)
    row_scale = lax.dynamic_slice_in_dim(row_scale, group_at * block_rows, block_rows)[None, :]
    col_scale = lax.dynamic_slice_in_dim(col_scale, slab_at * slab_width, slab_width)[:, None]

    def exchange(values, axis):
        return lax.all_to_all(values, axis, split_axis=0, concat_axis=0, tiled=True)

    chip_at = slab_at // 2
    lane = jnp.arange(slabs * rows, dtype=jnp.int32)
    away, within = lane // (2 * rows), lane % (2 * rows)
    part_at, within_part = away // (DIM_Z // 2), away % (DIM_Z // 2)
    chip_x = (chip_at // DIM_Z - part_at % DIM_X) % DIM_X
    chip_z = (chip_at % DIM_Z - within_part - part_at // DIM_X * (DIM_Z // 2)) % DIM_Z
    real = (chip_x * DIM_Z + chip_z) * 2 * rows + within
    to_real = (real[:, None] == lane[None, :]).astype(BF16)

    part = lax.all_to_all(tokens, "dp", split_axis=1, concat_axis=0, tiled=True)
    chip = chip_tokens(part.reshape(groups, rows, block_rows), core)
    old_weight, chip = in_order(old_weight, chip)
    along_z = [chip] + [lax.ppermute(chip, "tensor", shifted(0, k, 0)) for k in range(1, DIM_Z)]
    columns = grow_columns(old_weight, old_first, old_second, col_source, slabs, slab_width, groups, group_at)
    columns, *along_z = in_order(columns, *along_z)
    columns = exchange(columns, "tensor")

    def along_x(values):
        return [values] + [lax.ppermute(values, "tensor", shifted(k, 0, 0)) for k in range(1, DIM_X)]

    near = along_x(stacked(along_z[: DIM_Z // 2]))
    columns, row_scale, col_scale, place, *near = in_order(columns, row_scale, col_scale, place, *near)
    far = along_x(stacked(along_z[DIM_Z // 2 :]))
    grown = grow_rows(columns.reshape(old_width, LANES), row_source)
    blocks = exchange(grown.reshape(groups, block_rows, LANES), "dp")
    blocks, *far = in_order(blocks, *far)
    own = near + far
    parts = own + [lax.ppermute(values, "tensor", shifted(0, 0, 1)) for values in own]
    (weight,) = grown_block(weight_kernel, (blocks, row_scale, col_scale), 1, block_rows, slab_width, piece)

    terms = exchange(forward(place, parts, weight, groups), "dp")
    first, second = grown_block(moments_kernel, (blocks,), 2, block_rows, slab_width, piece)
    terms, first, second = in_order(terms, first, second)
    turned_grad = dot(cotangent.T, to_real.T)
    hidden = terms.astype(F32).sum(axis=0)
    activation = activate(hidden).astype(BF16)
    _, pullback = jax.vjp(activate, hidden)
    hidden_grad = pullback(turned_grad)[0].astype(BF16)
    activation = dot(activation, to_real).astype(BF16)

    grads = to_groups(hidden_grad)
    news = backward(place, parts, grads, first, second, weight)
    return (activation.T,) + tuple(new.T for new in news)


def solution(mesh):
    placed = (
        P(("dp", "tensor"), None),
        P("dp", "tensor"),
        P("tensor", None),
        P("tensor", None),
        P("tensor", None),
        P(),
        P(),
        P(),
        P(),
    )
    return jax.shard_map(
        shards,
        mesh=mesh,
        in_specs=placed,
        out_specs=(P("dp", "tensor"), P("dp", "tensor"), P("dp", "tensor"), P("dp", "tensor")),
        check_vma=False,
    )
```

```python
import functools

import jax
import jax.numpy as jnp
from jax import lax
from jax.experimental import pallas as pl
from jax.experimental.pallas import tpu as pltpu
from jax.sharding import PartitionSpec as P

beta_one = 0.9
beta_two = 0.95
adam_eps = 1e-08
learn_rate = 0.01
weight_decay = 0.1
adam_step = 1000.0

LANES = 128
F32 = jnp.float32
BF16 = jnp.bfloat16
VMEM_BYTES = 56 * 1024 * 1024


def growth_maps(row_source, col_source, row_level, col_level, old_width):
    identity = jnp.arange(old_width, dtype=jnp.int32)
    row_map = jnp.concatenate([identity, row_source])
    col_map = jnp.concatenate([identity, col_source])
    unit_scale = jnp.ones((old_width,), F32)
    row_scale = jnp.concatenate([unit_scale, (row_level.astype(F32) + 1.0) / 5.0])
    col_scale = jnp.concatenate([unit_scale, (col_level.astype(F32) + 1.0) / 5.0])
    return (row_map, col_map, row_scale, col_scale)


def activate(values):
    return jax.nn.gelu(values, approximate=True)


def chosen(index_row, depth, start=0):
    at = lax.broadcasted_iota(jnp.int32, (depth, index_row.shape[1]), 0) + start
    return jnp.where(at == index_row, 1.0, 0.0).astype(BF16)


def dot(a, b):
    return jnp.dot(a, b, preferred_element_type=F32)


def column_kernel(slabs_step, piece, copy_ref, own_ref, place_ref, *refs):
    sources, out_ref, total, own_place, held_refs, sems = refs[:3], refs[3], refs[4], refs[5], refs[6:9], refs[9]
    rows = total.shape[0] // 3
    depth = own_place.shape[1]
    steps = held_refs[0].shape[0]

    def copy(k, step):
        lanes = pl.ds(pl.multiple_of(step * depth, LANES), depth)
        return pltpu.make_async_copy(sources[k].at[:, lanes], held_refs[k].at[step], sems.at[k, step])

    for step in range(steps):
        for k in range(3):
            copy(k, step).start()
    for k in range(3):
        own_place[k] = chosen(own_ref[k : k + 1, :], depth)
    total[...] = jnp.zeros_like(total)

    def body(step, carry):
        for k in range(3):
            copy(k, step).wait()
        parts = [ref[step].astype(BF16) for ref in held_refs]
        same = functools.reduce(
            lambda a, b: a + b,
            [dot(part, own_place[k]) for k, part in enumerate(parts)],
        ).astype(BF16)
        for j in range(slabs_step):
            out_ref[step * slabs_step + j] = same[:, j * LANES : (j + 1) * LANES]
        total[...] += dot(jnp.concatenate(parts, axis=0), chosen(copy_ref[...], depth, step * depth))
        return carry

    lax.fori_loop(0, steps, body, 0)

    def finish():
        half = out_ref.shape[0] // 2
        width = total.shape[1]
        window = 2 * LANES
        held = [total[k * rows : (k + 1) * rows, :].astype(BF16) for k in range(3)]
        starts = [min(j * piece // LANES * LANES, width - window) for j in range(half)]
        for start in sorted(set(starts)):
            slabs = [j for j in range(half) if starts[j] == start]
            lanes = slice(slabs[0] * LANES, (slabs[-1] + 1) * LANES)
            spread = functools.reduce(
                lambda a, b: a + b,
                [
                    dot(part[:, start : start + window], chosen(place_ref[k : k + 1, lanes], window, start))
                    for k, part in enumerate(held)
                ],
            ).astype(BF16)
            for i, j in enumerate(slabs):
                out_ref[half + j] = spread[:, i * LANES : (i + 1) * LANES]

    finish()


def grow_columns(old_weight, old_first, old_second, col_source, slabs, slab_width, pieces, piece_at):
    rows, old_width = old_weight.shape
    piece = slab_width // pieces
    half = slabs // 2
    slabs_step = 2
    depth = slabs_step * slab_width
    copy_index = lax.dynamic_slice_in_dim(
        col_source.reshape(half, pieces, piece), piece_at, 1, 1
    ).reshape(1, half * piece)
    lane = jnp.arange(LANES, dtype=jnp.int32)[None, :] - piece * jnp.arange(3, dtype=jnp.int32)[:, None]
    inside = (lane >= 0) & (lane < piece)

    def spread_index(count, stride, offset):
        slab = jnp.arange(count, dtype=jnp.int32)[None, :, None] * stride + offset
        return jnp.where(inside[:, None, :], lane[:, None, :] + slab, -1).reshape(3, count * LANES)

    own_index = spread_index(slabs_step, slab_width, piece_at * piece)
    place_index = spread_index(half, piece, 0)
    return pl.pallas_call(
        functools.partial(column_kernel, slabs_step, piece),
        in_specs=[pl.BlockSpec(memory_space=pltpu.VMEM)] * 3 + [pl.BlockSpec(memory_space=pl.ANY)] * 3,
        out_specs=pl.BlockSpec(memory_space=pltpu.VMEM),
        out_shape=jax.ShapeDtypeStruct((slabs, rows, LANES), BF16),
        scratch_shapes=[
            pltpu.VMEM((3 * rows, half * piece), F32),
            pltpu.VMEM((3, depth, slabs_step * LANES), BF16),
            pltpu.VMEM((half // slabs_step, rows, depth), BF16),
            pltpu.VMEM((half // slabs_step, rows, depth), F32),
            pltpu.VMEM((half // slabs_step, rows, depth), F32),
            pltpu.SemaphoreType.DMA((3, half // slabs_step)),
        ],
        compiler_params=pltpu.CompilerParams(vmem_limit_bytes=VMEM_BYTES),
        cost_estimate=pl.CostEstimate(flops=1000, bytes_accessed=1000, transcendentals=0),
        name="grow_columns",
    )(copy_index, own_index, place_index, old_weight, old_first, old_second)


def row_kernel(index_ref, in_ref, out_ref, wide, picked):
    old = in_ref.shape[0]
    chunk = 512
    for c in range(0, old, chunk):
        part = in_ref[c : c + chunk, :]
        out_ref[c : c + chunk, :] = part
        wide[c : c + chunk, :] = part.astype(F32)

    def body(c, carry):
        for i in range(32):
            at = c * 32 + i
            picked[pl.ds(at, 1), :] = wide[pl.ds(index_ref[at], 1), :]
        return carry

    lax.fori_loop(0, old // 32, body, 0)
    for c in range(0, old, chunk):
        out_ref[old + c : old + c + chunk, :] = picked[c : c + chunk, :].astype(BF16)


def grow_rows(columns, row_source):
    old = columns.shape[0]
    return pl.pallas_call(
        row_kernel,
        in_specs=[
            pl.BlockSpec(memory_space=pltpu.SMEM),
            pl.BlockSpec(memory_space=pltpu.VMEM),
        ],
        out_specs=pl.BlockSpec(memory_space=pltpu.VMEM),
        out_shape=jax.ShapeDtypeStruct((2 * old, LANES), BF16),
        scratch_shapes=[pltpu.VMEM((old, LANES), F32), pltpu.VMEM((old, LANES), F32)],
        compiler_params=pltpu.CompilerParams(vmem_limit_bytes=VMEM_BYTES),
        cost_estimate=pl.CostEstimate(flops=1000, bytes_accessed=1000, transcendentals=0),
        name="grow_rows",
    )(row_source, columns)


def assemble(blocks_ref, array_at, piece, slab_width):
    pieces = blocks_ref.shape[0]
    row = lax.broadcasted_iota(jnp.int32, (slab_width, LANES), 0)
    at = lax.broadcasted_iota(jnp.int32, (slab_width, LANES), 1) - array_at * piece
    inside = (at >= 0) & (at < piece)
    place = jnp.concatenate(
        [jnp.where(inside & (d * piece + at == row), 1.0, 0.0).astype(BF16) for d in range(pieces)], axis=1
    )
    block = jnp.concatenate([blocks_ref[d] for d in range(pieces)], axis=1)
    return lax.dot_general(place, block, (((1,), (1,)), ((), ())), preferred_element_type=F32)


def moments_kernel(piece, blocks_ref, first_ref, second_ref):
    for a, ref in enumerate((first_ref, second_ref)):
        ref[...] = assemble(blocks_ref, a + 1, piece, ref.shape[0]).astype(BF16)


def grown_block(kernel, operands, results, block_rows, slab_width, piece):
    shape = jax.ShapeDtypeStruct((slab_width, block_rows), BF16)
    return pl.pallas_call(
        functools.partial(kernel, piece),
        in_specs=[pl.BlockSpec(memory_space=pltpu.VMEM)] * len(operands),
        out_specs=[pl.BlockSpec(memory_space=pltpu.VMEM)] * results,
        out_shape=[shape] * results,
        compiler_params=pltpu.CompilerParams(vmem_limit_bytes=VMEM_BYTES),
        cost_estimate=pl.CostEstimate(flops=1000, bytes_accessed=1000, transcendentals=0),
        name="grown_block_%d" % results,
    )(*operands)


def forward_kernel(count, piece, place_ref, *refs):
    parts, refs = refs[:count], refs[count:]
    blocks_ref, row_scale_ref, col_scale_ref, weight_ref, out_ref, held, sems = refs
    half = held.shape[0]
    core = place_ref[1]

    def copy(p, j):
        return pltpu.make_async_copy(parts[p].at[:, j], held.at[j, p], sems.at[j, p])

    for j in range(half):
        for p in range(count):
            copy(p, j).start()
    copied = assemble(blocks_ref, 0, piece, weight_ref.shape[0])
    weight_ref[...] = (copied * row_scale_ref[...] * col_scale_ref[...]).astype(BF16)

    def body(j, carry):
        for p in range(count):
            copy(p, j).wait()
        both = held[j].reshape(-1, weight_ref.shape[1])
        term = lax.dot_general(
            weight_ref[...], both, (((1,), (1,)), ((), ())), preferred_element_type=F32
        ).astype(BF16)
        width = out_ref.shape[2]
        out_ref[core * half + j] = term[:, :width]
        out_ref[(1 - core) * half + j] = term[:, width:]
        return carry

    lax.fori_loop(0, half, body, 0)


def forward(place, parts, blocks, row_scale, col_scale, groups, piece):
    near, half, chip_rows, block_rows = parts[0].shape
    slab_width = blocks.shape[0] * piece
    count = len(parts)
    shape = (groups, slab_width, count // 2 * near * chip_rows)
    vmem = pl.BlockSpec(memory_space=pltpu.VMEM)
    return pl.pallas_call(
        functools.partial(forward_kernel, count, piece),
        in_specs=[pl.BlockSpec(memory_space=pltpu.SMEM)]
        + [pl.BlockSpec(memory_space=pl.ANY)] * count
        + [vmem] * 3,
        out_specs=[vmem, vmem],
        out_shape=[
            jax.ShapeDtypeStruct((slab_width, block_rows), BF16),
            jax.ShapeDtypeStruct(shape, BF16),
        ],
        scratch_shapes=[
            pltpu.VMEM((half, count, near, chip_rows, block_rows), BF16),
            pltpu.SemaphoreType.DMA((half, count)),
        ],
        compiler_params=pltpu.CompilerParams(vmem_limit_bytes=VMEM_BYTES),
        cost_estimate=pl.CostEstimate(flops=1000, bytes_accessed=1000, transcendentals=0),
        name="forward_terms",
    )(place, *parts, blocks, row_scale, col_scale)


def adam_kernel(count, groups, place_ref, *refs):
    parts, grads, refs = refs[:count], refs[count : count + groups], refs[count + groups :]
    first_ref, second_ref, weight_ref = refs[:3]
    results, held, tokens, kept, in_sems, out_sems = refs[3:6], refs[6], refs[7], refs[8:11], refs[11], refs[12]
    steps, _, _, half, _, step_rows = tokens.shape
    core = place_ref[1]

    def columns(step):
        return pl.ds(pl.multiple_of(step * step_rows, LANES), step_rows)

    def copy_in(p, step):
        return pltpu.make_async_copy(parts[p].at[:, :, :, columns(step)], tokens.at[step, p], in_sems.at[step, p])

    def copy_out(k, step):
        return pltpu.make_async_copy(kept[k].at[step], results[k].at[:, columns(step)], out_sems.at[k, step])

    for step in range(steps):
        for p in range(count):
            copy_in(p, step).start()
    for k, ref in enumerate(grads):
        held[jnp.bitwise_xor(place_ref[0], k)] = ref[...]

    def body(step, carry):
        for p in range(count):
            copy_in(p, step).wait()
        grads_in_order, groups_in_order = [], []
        for mine, at in ((range(count // 2), core), (range(count // 2, count), 1 - core)):
            for j in range(half):
                grads_in_order.append(held[at * half + j])
                groups_in_order += [tokens[step, p, :, j].reshape(-1, step_rows) for p in mine]
        gradient = dot(jnp.concatenate(grads_in_order, axis=1), jnp.concatenate(groups_in_order, axis=0))
        weight = weight_ref[:, columns(step)].astype(F32)
        first = first_ref[:, columns(step)].astype(F32)
        second = second_ref[:, columns(step)].astype(F32)
        new_first = beta_one * first + (1.0 - beta_one) * gradient
        new_second = beta_two * second + (1.0 - beta_two) * gradient * gradient
        first_corr = 1.0 - beta_one**adam_step
        second_corr = 1.0 - beta_two**adam_step
        update = (
            new_first * (1.0 / first_corr) / (jnp.sqrt(new_second * (1.0 / second_corr)) + adam_eps)
            + weight_decay * weight
        )
        kept[0][step] = (weight - learn_rate * update).astype(BF16)
        kept[1][step] = new_first
        kept[2][step] = new_second
        for k in range(3):
            copy_out(k, step).start()
        return carry

    lax.fori_loop(0, steps, body, 0)
    for step in range(steps):
        for k in range(3):
            copy_out(k, step).wait()


def backward(place, parts, grads, first, second, weight):
    near, half, chip_rows, block_rows = parts[0].shape
    slab_width = weight.shape[0]
    step_rows = 256
    steps = block_rows // step_rows
    count, groups = len(parts), len(grads)
    vmem, anywhere = pl.BlockSpec(memory_space=pltpu.VMEM), pl.BlockSpec(memory_space=pl.ANY)
    kept = (steps, slab_width, step_rows)
    return pl.pallas_call(
        functools.partial(adam_kernel, count, groups),
        in_specs=[pl.BlockSpec(memory_space=pltpu.SMEM)] + [anywhere] * count + [vmem] * (groups + 3),
        out_specs=[anywhere] * 3,
        out_shape=[
            jax.ShapeDtypeStruct((slab_width, block_rows), BF16),
            jax.ShapeDtypeStruct((slab_width, block_rows), F32),
            jax.ShapeDtypeStruct((slab_width, block_rows), F32),
        ],
        scratch_shapes=[
            pltpu.VMEM((groups,) + grads[0].shape, BF16),
            pltpu.VMEM((steps, count, near, half, chip_rows, step_rows), BF16),
            pltpu.VMEM(kept, BF16),
            pltpu.VMEM(kept, F32),
            pltpu.VMEM(kept, F32),
            pltpu.SemaphoreType.DMA((steps, count)),
            pltpu.SemaphoreType.DMA((3, steps)),
        ],
        compiler_params=pltpu.CompilerParams(vmem_limit_bytes=VMEM_BYTES),
        cost_estimate=pl.CostEstimate(flops=1000, bytes_accessed=1000, transcendentals=0),
        name="gradient_adam",
    )(place, *parts, *grads, first, second, weight)


DIM_X, DIM_Z = 4, 4


def shifted(dx, dz, dc):
    places = [(x, z, c) for x in range(DIM_X) for z in range(DIM_Z) for c in range(2)]

    def at(x, z, c):
        return ((x % DIM_X) * DIM_Z + z % DIM_Z) * 2 + c % 2

    return [(at(x, z, c), at(x + dx, z + dz, c + dc)) for x, z, c in places]


def stack_kernel(*refs):
    for k, ref in enumerate(refs[:-1]):
        refs[-1][k] = ref[0]


def stacked(values):
    shape = (len(values),) + values[0].shape[1:]
    return pl.pallas_call(
        stack_kernel,
        in_specs=[pl.BlockSpec(memory_space=pltpu.VMEM)] * len(values),
        out_specs=pl.BlockSpec(memory_space=pltpu.VMEM),
        out_shape=jax.ShapeDtypeStruct(shape, values[0].dtype),
        compiler_params=pltpu.CompilerParams(vmem_limit_bytes=VMEM_BYTES),
        cost_estimate=pl.CostEstimate(flops=1000, bytes_accessed=1000, transcendentals=0),
        name="stack_tokens",
    )(*values)


def chip_tokens(part, core):
    groups, rows, block_rows = part.shape
    half = groups // 2
    mine = lax.dynamic_slice_in_dim(part, core * half, half, 0)
    away = lax.dynamic_slice_in_dim(part, (1 - core) * half, half, 0)
    theirs = lax.ppermute(away, "tensor", shifted(0, 0, 1))
    chip = jnp.stack([jnp.where(core == 0, mine, theirs), jnp.where(core == 0, theirs, mine)], axis=1)
    return chip.reshape(1, half, 2 * rows, block_rows)


def to_groups(values):
    groups = lax.axis_size("dp")
    return [values] + [lax.ppermute(values, "dp", [(i, i ^ k) for i in range(groups)]) for k in range(1, groups)]


def in_order(values, *others):
    return lax.optimization_barrier((values, *others))


def shards(tokens, cotangent, old_weight, old_first, old_second, row_source, col_source, row_level, col_level):
    slabs = lax.axis_size("tensor")
    groups = lax.axis_size("dp")
    slab_at, group_at = lax.axis_index("tensor"), lax.axis_index("dp")
    core = slab_at % 2
    place = jnp.stack([group_at, core]).astype(jnp.int32)
    rows = tokens.shape[0]
    old_width = old_weight.shape[1]
    new_width = old_width + row_source.shape[0]
    slab_width = new_width // slabs
    block_rows = new_width // groups
    piece = slab_width // groups
    _, _, row_scale, col_scale = growth_maps(row_source, col_source, row_level, col_level, old_width)
    row_scale = lax.dynamic_slice_in_dim(row_scale, group_at * block_rows, block_rows)[None, :]
    col_scale = lax.dynamic_slice_in_dim(col_scale, slab_at * slab_width, slab_width)[:, None]

    def exchange(values, axis):
        return lax.all_to_all(values, axis, split_axis=0, concat_axis=0, tiled=True)

    chip_at = slab_at // 2
    lane = jnp.arange(slabs * rows, dtype=jnp.int32)
    away, within = lane // (2 * rows), lane % (2 * rows)
    part_at, within_part = away // (DIM_Z // 2), away % (DIM_Z // 2)
    chip_x = (chip_at // DIM_Z - part_at % DIM_X) % DIM_X
    chip_z = (chip_at % DIM_Z - within_part - part_at // DIM_X * (DIM_Z // 2)) % DIM_Z
    real = (chip_x * DIM_Z + chip_z) * 2 * rows + within
    to_real = (real[:, None] == lane[None, :]).astype(BF16)

    part = lax.all_to_all(tokens, "dp", split_axis=1, concat_axis=0, tiled=True)
    chip = chip_tokens(part.reshape(groups, rows, block_rows), core)
    old_weight, chip = in_order(old_weight, chip)
    along_z = [chip] + [lax.ppermute(chip, "tensor", shifted(0, k, 0)) for k in range(1, DIM_Z)]
    columns = grow_columns(old_weight, old_first, old_second, col_source, slabs, slab_width, groups, group_at)
    columns, *along_z = in_order(columns, *along_z)
    columns = exchange(columns, "tensor")

    def along_x(values):
        return [values] + [lax.ppermute(values, "tensor", shifted(k, 0, 0)) for k in range(1, DIM_X)]

    near = along_x(stacked(along_z[: DIM_Z // 2]))
    columns, row_scale, col_scale, place, *near = in_order(columns, row_scale, col_scale, place, *near)
    far = along_x(stacked(along_z[DIM_Z // 2 :]))
    grown = grow_rows(columns.reshape(old_width, LANES), row_source)
    blocks = exchange(grown.reshape(groups, block_rows, LANES), "dp")
    own = near + far
    other = [lax.ppermute(values, "tensor", shifted(0, 0, 1)) for values in own]
    blocks, *parts = in_order(blocks, *own, *other)

    weight, terms = forward(place, parts, blocks, row_scale, col_scale, groups, piece)
    terms = exchange(terms, "dp")
    first, second = grown_block(moments_kernel, (blocks,), 2, block_rows, slab_width, piece)
    terms, first, second = in_order(terms, first, second)
    turned_grad = dot(cotangent.T, to_real.T)
    hidden = terms.astype(F32).sum(axis=0)
    activation = activate(hidden).astype(BF16)
    _, pullback = jax.vjp(activate, hidden)
    hidden_grad = pullback(turned_grad)[0].astype(BF16)
    activation = dot(activation, to_real).astype(BF16)

    grads = to_groups(hidden_grad)
    news = backward(place, parts, grads, first, second, weight)
    return (activation.T,) + tuple(new.T for new in news)


def solution(mesh):
    placed = (
        P(("dp", "tensor"), None),
        P("dp", "tensor"),
        P("tensor", None),
        P("tensor", None),
        P("tensor", None),
        P(),
        P(),
        P(),
        P(),
    )
    return jax.shard_map(
        shards,
        mesh=mesh,
        in_specs=placed,
        out_specs=(P("dp", "tensor"), P("dp", "tensor"), P("dp", "tensor"), P("dp", "tensor")),
        check_vma=False,
    )
```

```python
import functools

import jax
import jax.numpy as jnp
from jax import lax
from jax.experimental import pallas as pl
from jax.experimental.pallas import tpu as pltpu
from jax.sharding import PartitionSpec as P

beta_one = 0.9
beta_two = 0.95
adam_eps = 1e-08
learn_rate = 0.01
weight_decay = 0.1
adam_step = 1000.0

LANES = 128
F32 = jnp.float32
BF16 = jnp.bfloat16
VMEM_BYTES = 56 * 1024 * 1024


def growth_maps(row_source, col_source, row_level, col_level, old_width):
    identity = jnp.arange(old_width, dtype=jnp.int32)
    row_map = jnp.concatenate([identity, row_source])
    col_map = jnp.concatenate([identity, col_source])
    unit_scale = jnp.ones((old_width,), F32)
    row_scale = jnp.concatenate([unit_scale, (row_level.astype(F32) + 1.0) / 5.0])
    col_scale = jnp.concatenate([unit_scale, (col_level.astype(F32) + 1.0) / 5.0])
    return (row_map, col_map, row_scale, col_scale)


def activate(values):
    return jax.nn.gelu(values, approximate=True)


def chosen(index_row, depth, start=0):
    at = lax.broadcasted_iota(jnp.int32, (depth, index_row.shape[1]), 0) + start
    return jnp.where(at == index_row, 1.0, 0.0).astype(BF16)


def dot(a, b):
    return jnp.dot(a, b, preferred_element_type=F32)


def column_kernel(slabs_step, piece, copy_ref, own_ref, place_ref, *refs):
    sources, out_ref, total, own_place, held_refs, sems = refs[:3], refs[3], refs[4], refs[5], refs[6:9], refs[9]
    rows = total.shape[0] // 3
    depth = own_place.shape[1]
    steps = held_refs[0].shape[0]

    def copy(k, step):
        lanes = pl.ds(pl.multiple_of(step * depth, LANES), depth)
        return pltpu.make_async_copy(sources[k].at[:, lanes], held_refs[k].at[step], sems.at[k, step])

    for step in range(steps):
        for k in range(3):
            copy(k, step).start()
    for k in range(3):
        own_place[k] = chosen(own_ref[k : k + 1, :], depth)
    total[...] = jnp.zeros_like(total)

    def body(step, carry):
        for k in range(3):
            copy(k, step).wait()
        parts = [ref[step].astype(BF16) for ref in held_refs]
        same = functools.reduce(
            lambda a, b: a + b,
            [dot(part, own_place[k]) for k, part in enumerate(parts)],
        ).astype(BF16)
        for j in range(slabs_step):
            out_ref[step * slabs_step + j] = same[:, j * LANES : (j + 1) * LANES]
        total[...] += dot(jnp.concatenate(parts, axis=0), chosen(copy_ref[...], depth, step * depth))
        return carry

    lax.fori_loop(0, steps, body, 0)

    def finish():
        half = out_ref.shape[0] // 2
        width = total.shape[1]
        window = 2 * LANES
        held = [total[k * rows : (k + 1) * rows, :].astype(BF16) for k in range(3)]
        starts = [min(j * piece // LANES * LANES, width - window) for j in range(half)]
        for start in sorted(set(starts)):
            slabs = [j for j in range(half) if starts[j] == start]
            lanes = slice(slabs[0] * LANES, (slabs[-1] + 1) * LANES)
            spread = functools.reduce(
                lambda a, b: a + b,
                [
                    dot(part[:, start : start + window], chosen(place_ref[k : k + 1, lanes], window, start))
                    for k, part in enumerate(held)
                ],
            ).astype(BF16)
            for i, j in enumerate(slabs):
                out_ref[half + j] = spread[:, i * LANES : (i + 1) * LANES]

    finish()


def column_indices(col_source, slabs, slab_width, pieces, piece_at):
    piece = slab_width // pieces
    half = slabs // 2
    copy_index = lax.dynamic_slice_in_dim(
        col_source.reshape(half, pieces, piece), piece_at, 1, 1
    ).reshape(1, half * piece)
    lane = jnp.arange(LANES, dtype=jnp.int32)[None, :] - piece * jnp.arange(3, dtype=jnp.int32)[:, None]
    inside = (lane >= 0) & (lane < piece)

    def spread_index(count, stride, offset):
        slab = jnp.arange(count, dtype=jnp.int32)[None, :, None] * stride + offset
        return jnp.where(inside[:, None, :], lane[:, None, :] + slab, -1).reshape(3, count * LANES)

    return copy_index, spread_index(2, slab_width, piece_at * piece), spread_index(half, piece, 0)


def grow_columns(indices, old_weight, old_first, old_second, slabs, slab_width, pieces):
    rows = old_weight.shape[0]
    piece = slab_width // pieces
    half = slabs // 2
    slabs_step = 2
    depth = slabs_step * slab_width
    return pl.pallas_call(
        functools.partial(column_kernel, slabs_step, piece),
        in_specs=[pl.BlockSpec(memory_space=pltpu.VMEM)] * 3 + [pl.BlockSpec(memory_space=pl.ANY)] * 3,
        out_specs=pl.BlockSpec(memory_space=pltpu.VMEM),
        out_shape=jax.ShapeDtypeStruct((slabs, rows, LANES), BF16),
        scratch_shapes=[
            pltpu.VMEM((3 * rows, half * piece), F32),
            pltpu.VMEM((3, depth, slabs_step * LANES), BF16),
            pltpu.VMEM((half // slabs_step, rows, depth), BF16),
            pltpu.VMEM((half // slabs_step, rows, depth), F32),
            pltpu.VMEM((half // slabs_step, rows, depth), F32),
            pltpu.SemaphoreType.DMA((3, half // slabs_step)),
        ],
        compiler_params=pltpu.CompilerParams(vmem_limit_bytes=VMEM_BYTES),
        cost_estimate=pl.CostEstimate(flops=1000, bytes_accessed=1000, transcendentals=0),
        name="grow_columns",
    )(*indices, old_weight, old_first, old_second)


def row_kernel(index_ref, in_ref, out_ref, wide, picked):
    old = in_ref.shape[0]
    chunk = 512
    for c in range(0, old, chunk):
        part = in_ref[c : c + chunk, :]
        out_ref[c : c + chunk, :] = part
        wide[c : c + chunk, :] = part.astype(F32)

    def body(c, carry):
        for i in range(32):
            at = c * 32 + i
            picked[pl.ds(at, 1), :] = wide[pl.ds(index_ref[at], 1), :]
        return carry

    lax.fori_loop(0, old // 32, body, 0)
    for c in range(0, old, chunk):
        out_ref[old + c : old + c + chunk, :] = picked[c : c + chunk, :].astype(BF16)


def grow_rows(columns, row_source):
    old = columns.shape[0]
    return pl.pallas_call(
        row_kernel,
        in_specs=[
            pl.BlockSpec(memory_space=pltpu.SMEM),
            pl.BlockSpec(memory_space=pltpu.VMEM),
        ],
        out_specs=pl.BlockSpec(memory_space=pltpu.VMEM),
        out_shape=jax.ShapeDtypeStruct((2 * old, LANES), BF16),
        scratch_shapes=[pltpu.VMEM((old, LANES), F32), pltpu.VMEM((old, LANES), F32)],
        compiler_params=pltpu.CompilerParams(vmem_limit_bytes=16 * 1024 * 1024),
        cost_estimate=pl.CostEstimate(flops=1000, bytes_accessed=1000, transcendentals=0),
        name="grow_rows",
    )(row_source, columns)


def assemble(blocks_ref, array_at, piece, slab_width):
    pieces = blocks_ref.shape[0]
    row = lax.broadcasted_iota(jnp.int32, (slab_width, LANES), 0)
    at = lax.broadcasted_iota(jnp.int32, (slab_width, LANES), 1) - array_at * piece
    inside = (at >= 0) & (at < piece)
    place = jnp.concatenate(
        [jnp.where(inside & (d * piece + at == row), 1.0, 0.0).astype(BF16) for d in range(pieces)], axis=1
    )
    block = jnp.concatenate([blocks_ref[d] for d in range(pieces)], axis=1)
    return lax.dot_general(place, block, (((1,), (1,)), ((), ())), preferred_element_type=F32)


def moments_kernel(piece, blocks_ref, first_ref, second_ref):
    for a, ref in enumerate((first_ref, second_ref)):
        ref[...] = assemble(blocks_ref, a + 1, piece, ref.shape[0]).astype(BF16)


def grown_block(kernel, operands, results, block_rows, slab_width, piece):
    shape = jax.ShapeDtypeStruct((slab_width, block_rows), BF16)
    return pl.pallas_call(
        functools.partial(kernel, piece),
        in_specs=[pl.BlockSpec(memory_space=pltpu.VMEM)] * len(operands),
        out_specs=[pl.BlockSpec(memory_space=pltpu.VMEM)] * results,
        out_shape=[shape] * results,
        compiler_params=pltpu.CompilerParams(vmem_limit_bytes=VMEM_BYTES),
        cost_estimate=pl.CostEstimate(flops=1000, bytes_accessed=1000, transcendentals=0),
        name="grown_block_%d" % results,
    )(*operands)


def forward_kernel(count, piece, place_ref, *refs):
    parts, refs = refs[:count], refs[count:]
    blocks_ref, row_scale_ref, col_scale_ref, weight_ref, out_ref, held, sems = refs
    half = held.shape[0]
    core = place_ref[1]

    def copy(p, j):
        return pltpu.make_async_copy(parts[p].at[:, j], held.at[j, p], sems.at[j, p])

    for j in range(half):
        for p in range(count):
            copy(p, j).start()
    copied = assemble(blocks_ref, 0, piece, weight_ref.shape[0])
    weight_ref[...] = (copied * row_scale_ref[...] * col_scale_ref[...]).astype(BF16)

    def body(j, carry):
        for p in range(count):
            copy(p, j).wait()
        both = held[j].reshape(-1, weight_ref.shape[1])
        term = lax.dot_general(
            weight_ref[...], both, (((1,), (1,)), ((), ())), preferred_element_type=F32
        ).astype(BF16)
        width = out_ref.shape[2]
        out_ref[core * half + j] = term[:, :width]
        out_ref[(1 - core) * half + j] = term[:, width:]
        return carry

    lax.fori_loop(0, half, body, 0)


def forward(place, parts, blocks, row_scale, col_scale, groups, piece):
    near, half, chip_rows, block_rows = parts[0].shape
    slab_width = blocks.shape[0] * piece
    count = len(parts)
    shape = (groups, slab_width, count // 2 * near * chip_rows)
    vmem = pl.BlockSpec(memory_space=pltpu.VMEM)
    return pl.pallas_call(
        functools.partial(forward_kernel, count, piece),
        in_specs=[pl.BlockSpec(memory_space=pltpu.SMEM)]
        + [pl.BlockSpec(memory_space=pl.ANY)] * count
        + [vmem] * 3,
        out_specs=[vmem, vmem],
        out_shape=[
            jax.ShapeDtypeStruct((slab_width, block_rows), BF16),
            jax.ShapeDtypeStruct(shape, BF16),
        ],
        scratch_shapes=[
            pltpu.VMEM((half, count, near, chip_rows, block_rows), BF16),
            pltpu.SemaphoreType.DMA((half, count)),
        ],
        compiler_params=pltpu.CompilerParams(vmem_limit_bytes=VMEM_BYTES),
        cost_estimate=pl.CostEstimate(flops=1000, bytes_accessed=1000, transcendentals=0),
        name="forward_terms",
    )(place, *parts, blocks, row_scale, col_scale)


def adam_kernel(count, groups, place_ref, *refs):
    parts, grads, refs = refs[:count], refs[count : count + groups], refs[count + groups :]
    first_ref, second_ref, weight_ref = refs[:3]
    results, held, tokens, kept, in_sems, out_sems = refs[3:6], refs[6], refs[7], refs[8:11], refs[11], refs[12]
    steps, _, _, half, _, step_rows = tokens.shape
    core = place_ref[1]

    def columns(step):
        return pl.ds(pl.multiple_of(step * step_rows, LANES), step_rows)

    def copy_in(p, step):
        return pltpu.make_async_copy(parts[p].at[:, :, :, columns(step)], tokens.at[step, p], in_sems.at[step, p])

    def copy_out(k, step):
        return pltpu.make_async_copy(kept[k].at[step], results[k].at[:, columns(step)], out_sems.at[k, step])

    for step in range(steps):
        for p in range(count):
            copy_in(p, step).start()
    for k, ref in enumerate(grads):
        held[jnp.bitwise_xor(place_ref[0], k)] = ref[...]

    def body(step, carry):
        for p in range(count):
            copy_in(p, step).wait()
        grads_in_order, groups_in_order = [], []
        for mine, at in ((range(count // 2), core), (range(count // 2, count), 1 - core)):
            for j in range(half):
                grads_in_order.append(held[at * half + j])
                groups_in_order += [tokens[step, p, :, j].reshape(-1, step_rows) for p in mine]
        gradient = dot(jnp.concatenate(grads_in_order, axis=1), jnp.concatenate(groups_in_order, axis=0))
        weight = weight_ref[:, columns(step)].astype(F32)
        first = first_ref[:, columns(step)].astype(F32)
        second = second_ref[:, columns(step)].astype(F32)
        new_first = beta_one * first + (1.0 - beta_one) * gradient
        new_second = beta_two * second + (1.0 - beta_two) * gradient * gradient
        first_corr = 1.0 - beta_one**adam_step
        second_corr = 1.0 - beta_two**adam_step
        update = (
            new_first * (1.0 / first_corr) / (jnp.sqrt(new_second * (1.0 / second_corr)) + adam_eps)
            + weight_decay * weight
        )
        kept[0][step] = (weight - learn_rate * update).astype(BF16)
        kept[1][step] = new_first
        kept[2][step] = new_second
        for k in range(3):
            copy_out(k, step).start()
        return carry

    lax.fori_loop(0, steps, body, 0)
    for step in range(steps):
        for k in range(3):
            copy_out(k, step).wait()


def backward(place, parts, grads, first, second, weight):
    near, half, chip_rows, block_rows = parts[0].shape
    slab_width = weight.shape[0]
    step_rows = 256
    steps = block_rows // step_rows
    count, groups = len(parts), len(grads)
    vmem, anywhere = pl.BlockSpec(memory_space=pltpu.VMEM), pl.BlockSpec(memory_space=pl.ANY)
    kept = (steps, slab_width, step_rows)
    return pl.pallas_call(
        functools.partial(adam_kernel, count, groups),
        in_specs=[pl.BlockSpec(memory_space=pltpu.SMEM)] + [anywhere] * count + [vmem] * (groups + 3),
        out_specs=[anywhere] * 3,
        out_shape=[
            jax.ShapeDtypeStruct((slab_width, block_rows), BF16),
            jax.ShapeDtypeStruct((slab_width, block_rows), F32),
            jax.ShapeDtypeStruct((slab_width, block_rows), F32),
        ],
        scratch_shapes=[
            pltpu.VMEM((groups,) + grads[0].shape, BF16),
            pltpu.VMEM((steps, count, near, half, chip_rows, step_rows), BF16),
            pltpu.VMEM(kept, BF16),
            pltpu.VMEM(kept, F32),
            pltpu.VMEM(kept, F32),
            pltpu.SemaphoreType.DMA((steps, count)),
            pltpu.SemaphoreType.DMA((3, steps)),
        ],
        compiler_params=pltpu.CompilerParams(vmem_limit_bytes=VMEM_BYTES),
        cost_estimate=pl.CostEstimate(flops=1000, bytes_accessed=1000, transcendentals=0),
        name="gradient_adam",
    )(place, *parts, *grads, first, second, weight)


DIM_X, DIM_Z = 4, 4


def shifted(dx, dz, dc):
    places = [(x, z, c) for x in range(DIM_X) for z in range(DIM_Z) for c in range(2)]

    def at(x, z, c):
        return ((x % DIM_X) * DIM_Z + z % DIM_Z) * 2 + c % 2

    return [(at(x, z, c), at(x + dx, z + dz, c + dc)) for x, z, c in places]


def stack_kernel(*refs):
    for k, ref in enumerate(refs[:-1]):
        refs[-1][k] = ref[0]


def stacked(values):
    shape = (len(values),) + values[0].shape[1:]
    return pl.pallas_call(
        stack_kernel,
        in_specs=[pl.BlockSpec(memory_space=pltpu.VMEM)] * len(values),
        out_specs=pl.BlockSpec(memory_space=pltpu.VMEM),
        out_shape=jax.ShapeDtypeStruct(shape, values[0].dtype),
        compiler_params=pltpu.CompilerParams(vmem_limit_bytes=VMEM_BYTES),
        cost_estimate=pl.CostEstimate(flops=1000, bytes_accessed=1000, transcendentals=0),
        name="stack_tokens",
    )(*values)


def chip_tokens(part, core):
    groups, rows, block_rows = part.shape
    half = groups // 2
    mine = lax.dynamic_slice_in_dim(part, core * half, half, 0)
    away = lax.dynamic_slice_in_dim(part, (1 - core) * half, half, 0)
    theirs = lax.ppermute(away, "tensor", shifted(0, 0, 1))
    chip = jnp.stack([jnp.where(core == 0, mine, theirs), jnp.where(core == 0, theirs, mine)], axis=1)
    return chip.reshape(1, half, 2 * rows, block_rows)


def to_groups(values):
    groups = lax.axis_size("dp")
    return [values] + [lax.ppermute(values, "dp", [(i, i ^ k) for i in range(groups)]) for k in range(1, groups)]


def in_order(values, *others):
    return lax.optimization_barrier((values, *others))


def shards(tokens, cotangent, old_weight, old_first, old_second, row_source, col_source, row_level, col_level):
    slabs = lax.axis_size("tensor")
    groups = lax.axis_size("dp")
    slab_at, group_at = lax.axis_index("tensor"), lax.axis_index("dp")
    core = slab_at % 2
    place = jnp.stack([group_at, core]).astype(jnp.int32)
    rows = tokens.shape[0]
    old_width = old_weight.shape[1]
    new_width = old_width + row_source.shape[0]
    slab_width = new_width // slabs
    block_rows = new_width // groups
    piece = slab_width // groups
    _, _, row_scale, col_scale = growth_maps(row_source, col_source, row_level, col_level, old_width)
    row_scale = lax.dynamic_slice_in_dim(row_scale, group_at * block_rows, block_rows)[None, :]
    col_scale = lax.dynamic_slice_in_dim(col_scale, slab_at * slab_width, slab_width)[:, None]

    def exchange(values, axis):
        return lax.all_to_all(values, axis, split_axis=0, concat_axis=0, tiled=True)

    chip_at = slab_at // 2
    lane = jnp.arange(slabs * rows, dtype=jnp.int32)
    away, within = lane // (2 * rows), lane % (2 * rows)
    part_at, within_part = away // (DIM_Z // 2), away % (DIM_Z // 2)
    chip_x = (chip_at // DIM_Z - part_at % DIM_X) % DIM_X
    chip_z = (chip_at % DIM_Z - within_part - part_at // DIM_X * (DIM_Z // 2)) % DIM_Z
    real = (chip_x * DIM_Z + chip_z) * 2 * rows + within
    to_real = (real[:, None] == lane[None, :]).astype(BF16)

    part = lax.all_to_all(tokens, "dp", split_axis=1, concat_axis=0, tiled=True)
    indices = column_indices(col_source, slabs, slab_width, groups, group_at)
    part, *indices = in_order(part, *indices)
    chip = chip_tokens(part.reshape(groups, rows, block_rows), core)
    old_weight, chip = in_order(old_weight, chip)
    along_z = [chip] + [lax.ppermute(chip, "tensor", shifted(0, k, 0)) for k in range(1, DIM_Z)]
    columns = grow_columns(indices, old_weight, old_first, old_second, slabs, slab_width, groups)
    columns, *along_z = in_order(columns, *along_z)
    columns = exchange(columns, "tensor")

    def along_x(values):
        return [values] + [lax.ppermute(values, "tensor", shifted(k, 0, 0)) for k in range(1, DIM_X)]

    near = along_x(stacked(along_z[: DIM_Z // 2]))
    columns, row_scale, col_scale, place, *near = in_order(columns, row_scale, col_scale, place, *near)
    far = along_x(stacked(along_z[DIM_Z // 2 :]))
    grown = grow_rows(columns.reshape(old_width, LANES), row_source)
    blocks = exchange(grown.reshape(groups, block_rows, LANES), "dp")
    own = near + far
    other = [lax.ppermute(values, "tensor", shifted(0, 0, 1)) for values in own]
    blocks, *parts = in_order(blocks, *own, *other)

    weight, terms = forward(place, parts, blocks, row_scale, col_scale, groups, piece)
    terms = exchange(terms, "dp")
    first, second = grown_block(moments_kernel, (blocks,), 2, block_rows, slab_width, piece)
    terms, first, second = in_order(terms, first, second)
    turned_grad = dot(cotangent.T, to_real.T)
    hidden = terms.astype(F32).sum(axis=0)
    activation = activate(hidden).astype(BF16)
    _, pullback = jax.vjp(activate, hidden)
    hidden_grad = pullback(turned_grad)[0].astype(BF16)
    activation = dot(activation, to_real).astype(BF16)

    grads = to_groups(hidden_grad)
    news = backward(place, parts, grads, first, second, weight)
    return (activation.T,) + tuple(new.T for new in news)


def solution(mesh):
    placed = (
        P(("dp", "tensor"), None),
        P("dp", "tensor"),
        P("tensor", None),
        P("tensor", None),
        P("tensor", None),
        P(),
        P(),
        P(),
        P(),
    )
    return jax.shard_map(
        shards,
        mesh=mesh,
        in_specs=placed,
        out_specs=(P("dp", "tensor"), P("dp", "tensor"), P("dp", "tensor"), P("dp", "tensor")),
        check_vma=False,
    )
```
